32 devices in a mesh: frame: 8 (over z, y), head: 4 (over x, core).
Axes of the slice: x: 2, y: 2, z: 4, core: 2. Of those that a mesh axis runs over, the one named last changes fastest.
Arguments:
- q_raw: bfloat16 [2, 3072, 5120], P(None, 'frame', 'head'), may hold values from -200 to 200
- k_raw: bfloat16 [2, 3072, 5120], P(None, 'frame', 'head'), may hold values from -200 to 200
- v_in: bfloat16 [2, 3072, 5120], P(None, 'frame', 'head'), may hold values from -6 to 6
- cross_q_raw: bfloat16 [2, 3072, 5120], P(None, 'frame', 'head'), may hold values from -200 to 200
- text_k_raw: bfloat16 [2, 512, 5120], P(None, 'frame', 'head'), may hold values from -200 to 200
- text_v: bfloat16 [2, 512, 5120], P(None, 'frame', 'head'), may hold values from -6 to 6
- q_gain: float32 [5120], P('head'), may hold values from 0.5 to 1.5
- k_gain: float32 [5120], P('head'), may hold values from 0.5 to 1.5
- cross_q_gain: float32 [5120], P('head'), may hold values from 0.5 to 1.5
- text_k_gain: float32 [5120], P('head'), may hold values from 0.5 to 1.5
- nbr: int32 [24, 14], P('frame'), may hold values from 0 to 23, as said below
- nbr_count: int32 [24], P('frame'), may hold values from 7 to 14
- text_len: int32 [2], replicated, may hold values from 256 to 512
Outputs:
- self_out: bfloat16 [2, 3072, 5120], P(None, 'frame', 'head')
- cross_out: bfloat16 [2, 3072, 5120], P(None, 'frame', 'head')
The draws below stay inside these ranges and needn't reach their ends.
Inputs may be any that keep to these rules, and one draw needn't show every extreme that they name: Row r of nbr begins with r; its first nbr_count[r] entries are distinct tiles whose frame shard (tile // 3) lies at most 2 from that of r; its other entries equal r.
All inputs are finite; a program needn't handle non-finite values.
Results may differ from the reference program's by a relative error of at most 0.002.
The reference program's roundings to bfloat16 on the way (of `queries`, `key_rows`, `cross_queries`, `text_keys`, `self_weights` and `cross_weights`) count: a program that leaves them out, or rounds other values in their place, can miss the bound.
Values may be sent and summed in bfloat16 or wider, within the bound.
No kernel may reach another device: no remote copies, remote signals or barrier semaphores. Data moves between devices by JAX's collectives and lax.ppermute only.
A program may use at most 192 MiB of HBM per device.

```python
import math
import jax
import jax.numpy as jnp
from jax import lax

D = 5120
HEADS = 40
HD = 128
TXT = 512
TILE = 128
NB = 14
REACH = 2
TILES_DEV = 3
TILES = 24
TOKENS = 3072
N_FRAME = 8


def stream(key, label):
    return jax.random.fold_in(key, label)


def rough_rows(key, row_total, salt):
    column = jnp.arange(D, dtype=jnp.float32)
    column_scale = jnp.exp(column / D * math.log(3.0) + jax.random.uniform(stream(key, salt + 1), (D,), jnp.float32, 0.0, math.log(10.0)))
    row_scale = jnp.exp(jax.random.uniform(stream(key, salt + 2), (2, row_total, 1), jnp.float32, 0.0, math.log(10.0)))
    base = jnp.clip(jax.random.normal(stream(key, salt + 3), (2, row_total, D), jnp.float32), -6.0, 6.0)
    return 0.1 * base * column_scale * row_scale


def query_like(key, salt):
    field = rough_rows(key, TOKENS, salt)
    return field


def draw_q_raw(key, part):
    return query_like(key, 100).astype(jnp.bfloat16)


def draw_cross_q_raw(key, part):
    return query_like(key, 300).astype(jnp.bfloat16)


def draw_k_raw(key, part):
    field = rough_rows(key, TOKENS, 200)
    return field.astype(jnp.bfloat16)


def draw_text_k_raw(key, part):
    field = rough_rows(key, TXT, 400)
    return field.astype(jnp.bfloat16)


def tile_lists(key):
    reader = jnp.arange(TILES, dtype=jnp.int32)
    reader_shard = reader // TILES_DEV
    shard_steps = jnp.arange(2 * REACH + 1, dtype=jnp.int32) - REACH
    inner_tile = jnp.arange(TILES_DEV, dtype=jnp.int32)
    candidates_total = (2 * REACH + 1) * TILES_DEV
    candidate_shard = jnp.broadcast_to(reader_shard[:, None, None] + shard_steps[None, :, None], (TILES, 2 * REACH + 1, TILES_DEV))
    candidate = (candidate_shard * TILES_DEV + inner_tile[None, None, :]).reshape(TILES, candidates_total)
    usable = ((candidate_shard >= 0) & (candidate_shard < N_FRAME)).reshape(TILES, candidates_total) & (candidate != reader[:, None])
    ranking = jax.random.randint(stream(key, 501), (TILES, candidates_total), 0, 2 ** 20) * candidates_total + jnp.arange(candidates_total, dtype=jnp.int32)[None, :]
    ranking = jnp.where(usable, ranking, ranking + 2 ** 28)
    ranked_order = jnp.argsort(ranking, axis=1, stable=True)
    picked = jnp.take_along_axis(candidate, ranked_order[:, :NB - 1], axis=1)
    usable_count = jnp.sum(usable.astype(jnp.int32), axis=1)
    drawn_count = jax.random.randint(stream(key, 502), (TILES,), NB // 2, NB + 1)
    forced = (reader % 3 == 0) & (reader_shard >= REACH) & (reader_shard < N_FRAME - REACH)
    live_count = jnp.minimum(jnp.where(forced, NB, drawn_count), usable_count + 1).astype(jnp.int32)
    slot_index = jnp.arange(1, NB, dtype=jnp.int32)
    others_list = jnp.where(slot_index[None, :] < live_count[:, None], picked, reader[:, None])
    neighbour_list = jnp.concatenate([reader[:, None], others_list], axis=1).astype(jnp.int32)
    return (neighbour_list, live_count)


def draw_nbr(key, part):
    return tile_lists(key)[0]


def draw_nbr_count(key, part):
    return tile_lists(key)[1]


def block_levels(stream_key, extent, pieces, least, largest):
    level = 1.0
    for dim, parts in pieces:
        draws = jax.random.uniform(jax.random.fold_in(jax.random.fold_in(stream_key, 6), dim), (parts,), jnp.float32, least / len(pieces), largest / len(pieces))
        level = level * jnp.repeat(jnp.exp(draws), extent[dim] // parts).reshape((-1,) + (1,) * (len(extent) - 1 - dim))
    return level


def scatter_about(key, extent, scale, most, pieces=(), kind=jnp.bfloat16):
    loudness = block_levels(key, extent, pieces, -0.22, 0.18) if pieces else 1.0
    values = jax.random.normal(key, extent, jnp.float32) * scale * loudness
    return jnp.minimum(jnp.maximum(values, -most), most).astype(kind)


def setup_inputs(seed: int = 0) -> dict:
    key_of = jax.random.split(jax.random.key(seed), 14)
    return {
        "q_raw": draw_q_raw(jax.random.fold_in(key_of[13], 71), 0),
        "k_raw": draw_k_raw(jax.random.fold_in(key_of[13], 71), 0),
        "v_in": scatter_about(key_of[2], (2, TOKENS, D), 1.0, 6.0, ((1, 8), (2, 4))),
        "cross_q_raw": draw_cross_q_raw(jax.random.fold_in(key_of[13], 71), 0),
        "text_k_raw": draw_text_k_raw(jax.random.fold_in(key_of[13], 71), 0),
        "text_v": scatter_about(key_of[5], (2, TXT, D), 1.0, 6.0, ((1, 8), (2, 4))),
        "q_gain": jnp.clip(1.0 + 0.1 * jax.random.normal(key_of[6], (D,), jnp.float32), 0.5, 1.5),
        "k_gain": jnp.clip(1.0 + 0.1 * jax.random.normal(key_of[7], (D,), jnp.float32), 0.5, 1.5),
        "cross_q_gain": jnp.clip(1.0 + 0.1 * jax.random.normal(key_of[8], (D,), jnp.float32), 0.5, 1.5),
        "text_k_gain": jnp.clip(1.0 + 0.1 * jax.random.normal(key_of[9], (D,), jnp.float32), 0.5, 1.5),
        "nbr": draw_nbr(jax.random.fold_in(key_of[13], 71), 0),
        "nbr_count": draw_nbr_count(jax.random.fold_in(key_of[13], 71), 0),
        "text_len": jax.random.randint(key_of[12], (2,), TXT // 2, TXT + 1).astype(jnp.int32),
    }


EPSILON = 1e-06

def rms_scaled(tensor, gain_vector):
    values = tensor.astype(jnp.float32)
    mean_square = lax.optimization_barrier(jnp.mean(values * values, axis=-1, keepdims=True))
    return (values * lax.rsqrt(mean_square + EPSILON) * gain_vector).astype(jnp.bfloat16)

def soft_weights(scores):
    row_top = lax.optimization_barrier(jnp.max(scores, axis=-1, keepdims=True))
    powers = jnp.exp(scores - row_top)
    return (powers / lax.optimization_barrier(jnp.sum(powers, axis=-1, keepdims=True))).astype(jnp.bfloat16)

def reference(q_raw, k_raw, v_in, cross_q_raw, text_k_raw, text_v, q_gain, k_gain, cross_q_gain, text_k_gain, nbr, nbr_count, text_len):
    queries = rms_scaled(q_raw, q_gain)
    key_rows = rms_scaled(k_raw, k_gain)
    cross_queries = rms_scaled(cross_q_raw, cross_q_gain)
    text_keys = rms_scaled(text_k_raw, text_k_gain)
    score_scale = 1.0 / math.sqrt(HD)
    slot_tile = jnp.arange(NB * TILE, dtype=jnp.int32) // TILE
    text_mask = jnp.arange(TXT, dtype=jnp.int32)[None, :] < text_len[:, None]
    text_heads = text_keys.astype(jnp.float32).reshape(2, TXT, HEADS, HD)
    text_values = text_v.astype(jnp.float32).reshape(2, TXT, HEADS, HD)

    def take_tile(neighbour):
        row_start = neighbour * TILE
        return (lax.dynamic_slice_in_dim(key_rows, row_start, TILE, 1), lax.dynamic_slice_in_dim(v_in, row_start, TILE, 1))

    def one_tile(tile_index):
        row_start = tile_index * TILE
        query_rows = lax.dynamic_slice_in_dim(queries, row_start, TILE, 1).astype(jnp.float32).reshape(2, TILE, HEADS, HD)
        near_keys, near_values = jax.vmap(take_tile, out_axes=1)(nbr[tile_index])
        near_keys = near_keys.reshape(2, NB * TILE, HEADS, HD).astype(jnp.float32)
        near_values = near_values.reshape(2, NB * TILE, HEADS, HD).astype(jnp.float32)
        self_scores = jnp.einsum('cqhd,ckhd->chqk', query_rows, near_keys) * score_scale
        live_mask = slot_tile < nbr_count[tile_index]
        self_scores = jnp.where(live_mask[None, None, None, :], self_scores, -1e+30)
        self_weights = soft_weights(self_scores).astype(jnp.float32)
        self_rows = jnp.einsum('chqk,ckhd->cqhd', self_weights, near_values).astype(jnp.bfloat16).reshape(2, TILE, D)
        cross_rows_in = lax.dynamic_slice_in_dim(cross_queries, row_start, TILE, 1).astype(jnp.float32).reshape(2, TILE, HEADS, HD)
        cross_scores = jnp.einsum('cqhd,ckhd->chqk', cross_rows_in, text_heads) * score_scale
        cross_scores = jnp.where(text_mask[:, None, None, :], cross_scores, -1e+30)
        cross_weights = soft_weights(cross_scores).astype(jnp.float32)
        cross_rows = jnp.einsum('chqk,ckhd->cqhd', cross_weights, text_values).astype(jnp.bfloat16).reshape(2, TILE, D)
        return (self_rows, cross_rows)
    self_tiles, cross_tiles = lax.map(one_tile, jnp.arange(TILES, dtype=jnp.int32))
    self_out = jnp.transpose(self_tiles, (1, 0, 2, 3)).reshape(2, TOKENS, D)
    cross_out = jnp.transpose(cross_tiles, (1, 0, 2, 3)).reshape(2, TOKENS, D)
    return (self_out, cross_out)
```

```python
import functools
import math

import jax
import jax.numpy as jnp
from jax import lax
from jax.experimental import pallas as pl
from jax.experimental.pallas import tpu as pltpu
from jax.sharding import PartitionSpec as P

D = 5120
HD = 128
EPSILON = 1e-06
LEAST = 7
FAR = -1e30
SCALE2 = math.log2(math.e) / math.sqrt(HD)
VMEM = 56 * 1024 * 1024
BF = jnp.bfloat16
F32 = jnp.float32


def squares(tensor):
    values = tensor.astype(F32)
    return jnp.sum(values * values, axis=-1)


def weigh(stages, scratch):
    held = {}

    def scores(number):
        top, at, spans = None, 0, []
        for block in stages[number][0]:
            score = block()
            width = score.shape[1]
            scratch[number % 3, :, at : at + width] = score
            spans.append((at, width))
            at += width
            for c in range(0, width, 128):
                part = score[:, c : c + 128]
                top = part if top is None else jnp.maximum(top, part)
        held[number] = spans, jnp.max(top, axis=1, keepdims=True)

    def powers(number):
        spans, top = held[number]
        total = None
        for start, width in spans:
            for c in range(start, start + width, 128):
                power = jnp.exp2((scratch[number % 3, :, c : c + 128] - top) * SCALE2)
                scratch[number % 3, :, c : c + 128] = power
                total = power if total is None else total + power
        held[number] = spans, 1.0 / jnp.sum(total, axis=1, keepdims=True)

    def products(number):
        spans, inverse = held[number]
        out = None
        for (start, width), value in zip(spans, stages[number][1]):
            weights = (scratch[number % 3, :, start : start + width] * inverse).astype(BF)
            part = jnp.dot(weights, value(), preferred_element_type=F32)
            out = part if out is None else out + part
        stages[number][2](out.astype(BF))

    for step in range(len(stages) + 2):
        for work, number in ((scores, step), (powers, step - 1), (products, step - 2)):
            if 0 <= number < len(stages):
                work(number)


def pack_kernel(side, totals, gains, *refs):
    raws, outs = refs[:3], refs[3:]
    rows = raws[0].shape[1]
    width = raws[0].shape[2]

    def write(dest):
        for i in range(3):
            row = totals[0, i, :, :]
            factor = lax.rsqrt(row / D + EPSILON)
            column = jnp.transpose(jnp.broadcast_to(factor, (HD, rows)))
            for c in range(0, width, HD):
                value = raws[i][0, :, c : c + HD].astype(F32)
                dest[i][:, c : c + HD] = (value * column * gains[i : i + 1, c : c + HD]).astype(BF)

    @pl.when(pl.program_id(0) == 0)
    def _():
        write(outs[:3])

    @pl.when(pl.program_id(0) == 1)
    def _():
        write(outs[3:])


def pack(side, totals, gains, raws):
    tokens, width = raws[0].shape[1:]
    rows = 128
    steps = tokens // rows

    raw_spec = pl.BlockSpec((1, rows, width), lambda i, t, side_ref: ((side_ref[0] + i) % 2, t, 0))
    total_spec = pl.BlockSpec(
        (1, 3, 1, rows), lambda i, t, side_ref: ((side_ref[0] + i) % 2, 0, 0, t)
    )
    gain_spec = pl.BlockSpec(gains.shape, lambda i, t, side_ref: (0, 0))
    keep_spec = pl.BlockSpec((rows, width), lambda i, t, side_ref: (t * (1 - i) + (steps - 1) * i, 0))
    send_spec = pl.BlockSpec((rows, width), lambda i, t, side_ref: (t * i, 0))
    return pl.pallas_call(
        pack_kernel,
        grid_spec=pltpu.PrefetchScalarGridSpec(
            num_scalar_prefetch=1,
            grid=(2, steps),
            in_specs=[total_spec, gain_spec] + [raw_spec] * 3,
            out_specs=[keep_spec] * 3 + [send_spec] * 3,
        ),
        out_shape=[jax.ShapeDtypeStruct((tokens, width), BF)] * 6,
        compiler_params=pltpu.CompilerParams(vmem_limit_bytes=VMEM),
        cost_estimate=pl.CostEstimate(
            flops=0, bytes_accessed=12 * tokens * width * 2, transcendentals=0
        ),
        name="norm_pack",
    )(side, totals, gains, *raws)


def join_kernel(first, second, *outs, spans):
    for i, ref in enumerate((first, second)):

        @pl.when(pl.program_id(0) == i)
        def _(ref=ref):
            for out, (c0, c1) in zip(outs, spans):
                out[...] = ref[:, c0:c1]


def join(first, second, spans):
    tokens, width = first.shape
    return pl.pallas_call(
        functools.partial(join_kernel, spans=spans),
        grid=(2,),
        in_specs=[pl.BlockSpec((tokens, width), lambda i: (0, 0))] * 2,
        out_specs=[pl.BlockSpec((tokens, c1 - c0), lambda i: (i, 0)) for c0, c1 in spans],
        out_shape=[jax.ShapeDtypeStruct((2 * tokens, c1 - c0), BF) for c0, c1 in spans],
        compiler_params=pltpu.CompilerParams(vmem_limit_bytes=VMEM),
        cost_estimate=pl.CostEstimate(
            flops=0, bytes_accessed=4 * tokens * width * 2, transcendentals=0
        ),
        name="join",
    )(first, second)


def self_kernel(index, count, *refs, tile, slots, n_k, n_v):
    k_pieces, v_pieces = refs[:n_k], refs[n_k : n_k + n_v]
    q_pieces, out_pieces = refs[n_k + n_v : n_k + n_v + 2], refs[n_k + n_v + 2 : n_k + n_v + 4]
    k_window, v_window, scratch = refs[n_k + n_v + 4 :]
    at = 0
    for piece in k_pieces:
        for start in range(0, piece.shape[0], tile):
            k_window[at] = jnp.transpose(piece[start : start + tile, :])
            at += 1
    at = 0
    for piece in v_pieces:
        for start in range(0, piece.shape[0], tile):
            v_window[at] = piece[start : start + tile, :]
            at += 1
    readers = q_pieces[0].shape[0] // tile
    column = lax.broadcasted_iota(jnp.int32, (1, 2 * tile), 1)

    def stage(half, r):
        number = half * readers + r
        live = count[number]
        rows = slice(r * tile, (r + 1) * tile)

        def block(slot):
            pair = [k_window[index[number * slots + slot + i]] for i in range(2)]
            score = jnp.dot(
                q_pieces[half][rows, :],
                jnp.concatenate(pair, axis=1),
                preferred_element_type=F32,
            )
            if slot + 1 >= LEAST:
                score = jnp.where(column < (live - slot) * tile, score, FAR)
            return score

        def value(slot):
            pair = [v_window[index[number * slots + slot + i]] for i in range(2)]
            return jnp.concatenate(pair, axis=0)

        def store(out):
            out_pieces[half][rows, :] = out

        return (
            [functools.partial(block, slot) for slot in range(0, slots, 2)],
            [functools.partial(value, slot) for slot in range(0, slots, 2)],
            store,
        )

    weigh([stage(half, r) for half in range(2) for r in range(readers)], scratch)


def self_attention(index, count, k_pieces, v_pieces, q_pieces, first_head, tile, slots):
    tokens = q_pieces[0].shape[0]
    width = k_pieces[0].shape[1]
    heads = width // HD
    window = 6 * tokens // tile

    def spec(piece, base):
        return pl.BlockSpec((piece.shape[0], HD), lambda h, *_: (0, h + base))

    rows = 2 * tokens * heads
    return pl.pallas_call(
        functools.partial(
            self_kernel, tile=tile, slots=slots, n_k=len(k_pieces), n_v=len(v_pieces)
        ),
        grid_spec=pltpu.PrefetchScalarGridSpec(
            num_scalar_prefetch=2,
            grid=(heads,),
            in_specs=[spec(piece, 0) for piece in k_pieces]
            + [spec(piece, first_head) for piece in (*v_pieces, *q_pieces)],
            out_specs=[pl.BlockSpec((tokens, HD), lambda h, *_: (0, h))] * 2,
            scratch_shapes=[
                pltpu.VMEM((window, HD, tile), BF),
                pltpu.VMEM((window, tile, HD), BF),
                pltpu.VMEM((3, tile, slots * tile), F32),
            ],
        ),
        out_shape=[jax.ShapeDtypeStruct((tokens, width), BF)] * 2,
        compiler_params=pltpu.CompilerParams(vmem_limit_bytes=VMEM),
        cost_estimate=pl.CostEstimate(
            flops=rows * slots * tile * HD * 4 * 2,
            bytes_accessed=16 * tokens * width * 2,
            transcendentals=rows * slots * tile,
        ),
        name="self_attention",
    )(index, count, *k_pieces, *v_pieces, *q_pieces)


def cross_kernel(place, *refs, n_text, text_total, order):
    text = refs[:n_text]
    q_pieces = refs[n_text : n_text + 2]
    out_pieces = refs[n_text + 2 : n_text + 4]
    window, turned, scratch = refs[n_text + 4 :]
    at = 0
    for ref in text:
        rows = ref.shape[1]
        window[:, at : at + rows, :] = ref[...]
        at += rows
    start = pl.multiple_of(place[0], order)
    live = place[1]
    side = place[2]
    tokens = q_pieces[0].shape[0]
    block_rows = scratch.shape[1]
    turned[...] = jnp.transpose(window[0, pl.ds(start, text_total), :])
    column = lax.broadcasted_iota(jnp.int32, (1, text_total), 1)
    half = order // 2
    seen = jnp.where(side == 1, column ^ half, column) < live
    span = 256

    def stage(part, r):
        rows = slice(r * block_rows, (r + 1) * block_rows)

        def block(c):
            score = jnp.dot(
                q_pieces[part][rows, :], turned[:, c : c + span], preferred_element_type=F32
            )
            return jnp.where(seen[:, c : c + span], score, FAR)

        def value(c):
            return window[1, pl.ds(pl.multiple_of(start + c, order), span), :]

        def store(out):
            out_pieces[part][rows, :] = out

        return (
            [functools.partial(block, c) for c in range(0, text_total, span)],
            [functools.partial(value, c) for c in range(0, text_total, span)],
            store,
        )

    weigh([stage(part, r) for part in range(2) for r in range(tokens // block_rows)], scratch)


def cross_attention(place, text, q_pieces, text_total, order):
    tokens, width = q_pieces[0].shape
    heads = width // HD
    window_rows = sum(block.shape[1] for block in text)
    block_rows = tokens // 2
    spec = pl.BlockSpec((tokens, HD), lambda h, *_: (0, h))
    text_specs = [pl.BlockSpec((2, block.shape[1], HD), lambda h, *_: (0, 0, h)) for block in text]
    rows = 2 * tokens * heads
    return pl.pallas_call(
        functools.partial(cross_kernel, n_text=len(text), text_total=text_total, order=order),
        grid_spec=pltpu.PrefetchScalarGridSpec(
            num_scalar_prefetch=1,
            grid=(heads,),
            in_specs=text_specs + [spec] * 2,
            out_specs=[spec] * 2,
            scratch_shapes=[
                pltpu.VMEM((2, window_rows, HD), BF),
                pltpu.VMEM((HD, text_total), BF),
                pltpu.VMEM((3, block_rows, text_total), F32),
            ],
        ),
        out_shape=[jax.ShapeDtypeStruct((tokens, width), BF)] * 2,
        compiler_params=pltpu.CompilerParams(vmem_limit_bytes=VMEM),
        cost_estimate=pl.CostEstimate(
            flops=rows * text_total * HD * 4 * 2,
            bytes_accessed=4 * tokens * width * 2 + 2 * window_rows * width * 2,
            transcendentals=rows * text_total,
        ),
        name="cross_attention",
    )(place, *text, *q_pieces)


def body(
    q_raw,
    k_raw,
    v_in,
    cross_q_raw,
    text_k_raw,
    text_v,
    q_gain,
    k_gain,
    cross_q_gain,
    text_k_gain,
    nbr,
    nbr_count,
    text_len,
):
    tokens, width = q_raw.shape[1:]
    heads = width // HD
    tiles = nbr.shape[0]
    slots = nbr.shape[1]
    tile = tokens // tiles
    shards = lax.axis_size("frame")
    pairs = shards // 2
    shard = lax.axis_index("frame")
    side = shard % 2
    pair = shard // 2
    cuts = [0, (2 * heads + 4) // 5, (7 * heads + 9) // 10, heads]
    chunks = [(a * HD, b * HD) for a, b in zip(cuts, cuts[1:])]

    def partner(value):
        return lax.ppermute(value, "frame", [(i, i ^ 1) for i in range(shards)])

    def up(value, least=0):
        moves = [(i, i + 2) for i in range(shards - 2) if i // 2 >= least]
        return lax.ppermute(value, "frame", moves)

    def down(value, least=0):
        moves = [(i, i - 2) for i in range(2, shards) if i // 2 < pairs - least]
        return lax.ppermute(value, "frame", moves)

    def mine(value):
        return lax.dynamic_index_in_dim(value, side, 0, keepdims=False)

    def theirs(value):
        return lax.dynamic_index_in_dim(value, 1 - side, 0, keepdims=False)

    def after(value, *others):
        return lax.optimization_barrier((value, *others))[0]

    meta = jnp.concatenate([nbr, nbr_count[:, None]], axis=1)
    got_meta = partner(meta)
    meta = jnp.concatenate([meta, got_meta], axis=0)
    neighbour, count = meta[:, :slots], meta[:, slots]
    near_shard = neighbour // tiles
    index = (
        (near_shard // 2 - pair + 1) * (2 * tiles)
        + ((near_shard % 2) ^ side) * tiles
        + neighbour % tiles
    )
    index = jnp.clip(index, 0, 6 * tiles - 1).reshape(-1)
    v_keep, v_send = mine(v_in), theirs(v_in)
    v_got = partner(v_send)
    v_up, v_down = up(v_keep), down(v_keep)

    q_late, k_late, cq_late, text_late = (
        after(t, v_keep, v_send) for t in (q_raw, k_raw, cross_q_raw, text_k_raw)
    )
    sums = jnp.concatenate([squares(t) for t in (q_late, k_late, cq_late, text_late)], axis=1)
    totals = lax.psum(sums, "head")
    v_got_up, v_got_down = up(v_got), down(v_got)
    v_pieces = [v_up, v_got_up, v_keep, v_got, v_down, v_got_down]

    text_factor = lax.rsqrt(totals[:, 3 * tokens :] / D + EPSILON)[:, :, None]
    text_keys = (text_k_raw.astype(F32) * text_factor * text_k_gain).astype(BF)
    shard_text = text_keys.shape[1]
    text_total = shard_text * shards
    text_both = jnp.stack([text_keys, text_v], axis=1)
    order = 2 * shard_text
    relayed = pairs <= 4
    if relayed:
        text_got = partner(after(theirs(text_both), v_got))
        text_pair = jnp.concatenate([mine(text_both), text_got], axis=1)
        start, text_side = (pairs - 1 - pair) * order, side
    else:
        gathered = lax.all_gather(text_both, "frame", axis=2, tiled=True)
        text_got = mine(gathered)
        start, text_side = jnp.zeros_like(pair), jnp.zeros_like(side)
    place = jnp.stack([start, text_len[side], text_side]).astype(jnp.int32)

    keep_q, keep_k, keep_cq, send_q, send_k, send_cq = pack(
        jnp.reshape(side, (1,)),
        after(totals[:, : 3 * tokens].reshape(2, 3, 1, tokens), v_got, got_meta),
        jnp.stack([q_gain, k_gain, cross_q_gain]),
        (q_raw, k_raw, cross_q_raw),
    )
    got_cq = partner(after(send_cq, v_up, v_down))
    got_k = partner(after(send_k, text_got, v_got_up, v_got_down))
    got_q = partner(after(send_q, got_cq))
    cross_pieces = [keep_cq, got_cq]
    q_pieces = [keep_q, got_q]

    if relayed:
        text_pair = after(text_pair, v_up, v_down)
        ups, downs = [text_pair], [text_pair]
        for step in range(pairs - 1):
            ups.append(up(ups[-1], step))
            downs.append(down(downs[-1], step))
        text = ups[:0:-1] + [text_pair] + downs[1:]
    else:
        text = [text_got]
    joined_k = join(keep_k, got_k, chunks)
    k_pieces = []
    for number, own in enumerate(joined_k):
        if number < 2:
            own = after(own, *text[max(0, 1 - number) : len(text) - max(0, 1 - number)])
        else:
            own = after(own, *k_pieces[number - 2])
        k_pieces.append([up(own), own, down(own)])

    cross_keep, cross_send = cross_attention(place, text, cross_pieces, text_total, order)
    cross_got = partner(after(cross_send, got_q))
    self_keep, self_got = [], []
    for number, chunk in enumerate(chunks):
        out_keep, out_send = self_attention(
            index,
            count,
            [after(k, cross_keep, *self_keep) for k in k_pieces[number]],
            v_pieces,
            q_pieces,
            chunk[0] // HD,
            tile,
            slots,
        )
        self_keep.append(out_keep)
        self_got.append(partner(out_send))

    def joined(own, got):
        rows = jnp.arange(2, dtype=jnp.int32)[:, None, None] == side
        return jnp.where(rows, own[None], got[None])

    self_out = jnp.concatenate([joined(a, b) for a, b in zip(self_keep, self_got)], axis=2)
    return (self_out, joined(cross_keep, cross_got))


def solution(mesh):
    in_specs = (
        P(None, "frame", "head"),
        P(None, "frame", "head"),
        P(None, "frame", "head"),
        P(None, "frame", "head"),
        P(None, "frame", "head"),
        P(None, "frame", "head"),
        P("head"),
        P("head"),
        P("head"),
        P("head"),
        P("frame", None),
        P("frame"),
        P(),
    )
    out_specs = (P(None, "frame", "head"), P(None, "frame", "head"))
    return jax.shard_map(body, mesh=mesh, in_specs=in_specs, out_specs=out_specs, check_vma=False)
```

```python
import functools
import math

import jax
import jax.numpy as jnp
from jax import lax
from jax.experimental import pallas as pl
from jax.experimental.pallas import tpu as pltpu
from jax.sharding import PartitionSpec as P

D = 5120
HD = 128
EPSILON = 1e-06
LEAST = 7
FAR = -1e30
SCALE2 = math.log2(math.e) / math.sqrt(HD)
VMEM = 56 * 1024 * 1024
BF = jnp.bfloat16
BRIEF = pl.CostEstimate(flops=0, bytes_accessed=1024, transcendentals=0)
F32 = jnp.float32


def squares(tensor):
    values = tensor.astype(F32)
    return jnp.sum(values * values, axis=-1)


def weigh(stages, scratch):
    held = {}

    def scores(number):
        top, at, spans = None, 0, []
        for block in stages[number][0]:
            score = block()
            width = score.shape[1]
            scratch[number % 3, :, at : at + width] = score
            spans.append((at, width))
            at += width
            for c in range(0, width, 128):
                part = score[:, c : c + 128]
                top = part if top is None else jnp.maximum(top, part)
        held[number] = spans, jnp.max(top, axis=1, keepdims=True)

    def powers(number):
        spans, top = held[number]
        total = None
        for start, width in spans:
            for c in range(start, start + width, 128):
                power = jnp.exp2((scratch[number % 3, :, c : c + 128] - top) * SCALE2)
                scratch[number % 3, :, c : c + 128] = power
                total = power if total is None else total + power
        held[number] = spans, 1.0 / jnp.sum(total, axis=1, keepdims=True)

    def products(number):
        spans, inverse = held[number]
        out = None
        for (start, width), value in zip(spans, stages[number][1]):
            weights = (scratch[number % 3, :, start : start + width] * inverse).astype(BF)
            part = jnp.dot(weights, value(), preferred_element_type=F32)
            out = part if out is None else out + part
        stages[number][2](out.astype(BF))

    for step in range(len(stages) + 2):
        for work, number in ((scores, step), (powers, step - 1), (products, step - 2)):
            if 0 <= number < len(stages):
                work(number)


def pack_kernel(side, totals, gains, *refs):
    raws, outs = refs[:3], refs[3:]
    rows = raws[0].shape[1]
    width = raws[0].shape[2]

    def write(dest):
        for i in range(3):
            row = totals[0, i, :, :]
            factor = lax.rsqrt(row / D + EPSILON)
            column = jnp.transpose(jnp.broadcast_to(factor, (HD, rows)))
            for c in range(0, width, HD):
                value = raws[i][0, :, c : c + HD].astype(F32)
                dest[i][:, c : c + HD] = (value * column * gains[i : i + 1, c : c + HD]).astype(BF)

    @pl.when(pl.program_id(0) == 0)
    def _():
        write(outs[:3])

    @pl.when(pl.program_id(0) == 1)
    def _():
        write(outs[3:])


def pack(side, totals, gains, raws):
    tokens, width = raws[0].shape[1:]
    rows = 128
    steps = tokens // rows

    raw_spec = pl.BlockSpec((1, rows, width), lambda i, t, side_ref: ((side_ref[0] + i) % 2, t, 0))
    total_spec = pl.BlockSpec(
        (1, 3, 1, rows), lambda i, t, side_ref: ((side_ref[0] + i) % 2, 0, 0, t)
    )
    gain_spec = pl.BlockSpec(gains.shape, lambda i, t, side_ref: (0, 0))
    keep_spec = pl.BlockSpec((rows, width), lambda i, t, side_ref: (t * (1 - i) + (steps - 1) * i, 0))
    send_spec = pl.BlockSpec((rows, width), lambda i, t, side_ref: (t * i, 0))
    return pl.pallas_call(
        pack_kernel,
        grid_spec=pltpu.PrefetchScalarGridSpec(
            num_scalar_prefetch=1,
            grid=(2, steps),
            in_specs=[total_spec, gain_spec] + [raw_spec] * 3,
            out_specs=[keep_spec] * 3 + [send_spec] * 3,
        ),
        out_shape=[jax.ShapeDtypeStruct((tokens, width), BF)] * 6,
        compiler_params=pltpu.CompilerParams(vmem_limit_bytes=VMEM),
        cost_estimate=BRIEF,
        name="norm_pack",
    )(side, totals, gains, *raws)


def join_kernel(first, second, *outs, spans):
    for i, ref in enumerate((first, second)):

        @pl.when(pl.program_id(0) == i)
        def _(ref=ref):
            for out, (c0, c1) in zip(outs, spans):
                out[...] = ref[:, c0:c1]


def join(first, second, spans):
    tokens, width = first.shape
    return pl.pallas_call(
        functools.partial(join_kernel, spans=spans),
        grid=(2,),
        in_specs=[pl.BlockSpec((tokens, width), lambda i: (0, 0))] * 2,
        out_specs=[pl.BlockSpec((tokens, c1 - c0), lambda i: (i, 0)) for c0, c1 in spans],
        out_shape=[jax.ShapeDtypeStruct((2 * tokens, c1 - c0), BF) for c0, c1 in spans],
        compiler_params=pltpu.CompilerParams(vmem_limit_bytes=VMEM),
        cost_estimate=BRIEF,
        name="join",
    )(first, second)


def self_kernel(index, count, *refs, tile, slots, n_k, n_v):
    k_pieces, v_pieces = refs[:n_k], refs[n_k : n_k + n_v]
    q_pieces, out_pieces = refs[n_k + n_v : n_k + n_v + 2], refs[n_k + n_v + 2 : n_k + n_v + 4]
    k_window, v_window, scratch = refs[n_k + n_v + 4 :]
    at = 0
    for piece in k_pieces:
        for start in range(0, piece.shape[0], tile):
            k_window[at] = jnp.transpose(piece[start : start + tile, :])
            at += 1
    at = 0
    for piece in v_pieces:
        for start in range(0, piece.shape[0], tile):
            v_window[at] = piece[start : start + tile, :]
            at += 1
    readers = q_pieces[0].shape[0] // tile
    column = lax.broadcasted_iota(jnp.int32, (1, 2 * tile), 1)

    def stage(half, r):
        number = half * readers + r
        live = count[number]
        rows = slice(r * tile, (r + 1) * tile)

        def block(slot):
            pair = [k_window[index[number * slots + slot + i]] for i in range(2)]
            score = jnp.dot(
                q_pieces[half][rows, :],
                jnp.concatenate(pair, axis=1),
                preferred_element_type=F32,
            )
            if slot + 1 >= LEAST:
                score = jnp.where(column < (live - slot) * tile, score, FAR)
            return score

        def value(slot):
            pair = [v_window[index[number * slots + slot + i]] for i in range(2)]
            return jnp.concatenate(pair, axis=0)

        def store(out):
            out_pieces[half][rows, :] = out

        return (
            [functools.partial(block, slot) for slot in range(0, slots, 2)],
            [functools.partial(value, slot) for slot in range(0, slots, 2)],
            store,
        )

    weigh([stage(half, r) for half in range(2) for r in range(readers)], scratch)


def self_attention(index, count, k_pieces, v_pieces, q_pieces, first_head, k_head, heads, tile, slots):
    tokens = q_pieces[0].shape[0]
    width = heads * HD
    window = 6 * tokens // tile

    def spec(piece, base):
        return pl.BlockSpec((piece.shape[0], HD), lambda h, *_: (0, h + base))

    rows = 2 * tokens * heads
    return pl.pallas_call(
        functools.partial(
            self_kernel, tile=tile, slots=slots, n_k=len(k_pieces), n_v=len(v_pieces)
        ),
        grid_spec=pltpu.PrefetchScalarGridSpec(
            num_scalar_prefetch=2,
            grid=(heads,),
            in_specs=[spec(piece, k_head) for piece in k_pieces]
            + [spec(piece, first_head) for piece in (*v_pieces, *q_pieces)],
            out_specs=[pl.BlockSpec((tokens, HD), lambda h, *_: (0, h))] * 2,
            scratch_shapes=[
                pltpu.VMEM((window, HD, tile), BF),
                pltpu.VMEM((window, tile, HD), BF),
                pltpu.VMEM((3, tile, slots * tile), F32),
            ],
        ),
        out_shape=[jax.ShapeDtypeStruct((tokens, width), BF)] * 2,
        compiler_params=pltpu.CompilerParams(vmem_limit_bytes=VMEM),
        cost_estimate=pl.CostEstimate(
            flops=rows * slots * tile * HD * 4 * 2,
            bytes_accessed=16 * tokens * width * 2,
            transcendentals=rows * slots * tile,
        ),
        name="self_attention",
    )(index, count, *k_pieces, *v_pieces, *q_pieces)


def cross_kernel(place, *refs, n_text, text_total, order):
    text = refs[:n_text]
    q_pieces = refs[n_text : n_text + 2]
    out_pieces = refs[n_text + 2 : n_text + 4]
    window, turned, scratch = refs[n_text + 4 :]
    at = 0
    for ref in text:
        rows = ref.shape[1]
        window[:, at : at + rows, :] = ref[...]
        at += rows
    start = pl.multiple_of(place[0], order)
    live = place[1]
    side = place[2]
    tokens = q_pieces[0].shape[0]
    block_rows = scratch.shape[1]
    turned[...] = jnp.transpose(window[0, pl.ds(start, text_total), :])
    column = lax.broadcasted_iota(jnp.int32, (1, text_total), 1)
    half = order // 2
    seen = jnp.where(side == 1, column ^ half, column) < live
    span = 256

    def stage(part, r):
        rows = slice(r * block_rows, (r + 1) * block_rows)

        def block(c):
            score = jnp.dot(
                q_pieces[part][rows, :], turned[:, c : c + span], preferred_element_type=F32
            )
            return jnp.where(seen[:, c : c + span], score, FAR)

        def value(c):
            return window[1, pl.ds(pl.multiple_of(start + c, order), span), :]

        def store(out):
            out_pieces[part][rows, :] = out

        return (
            [functools.partial(block, c) for c in range(0, text_total, span)],
            [functools.partial(value, c) for c in range(0, text_total, span)],
            store,
        )

    weigh([stage(part, r) for part in range(2) for r in range(tokens // block_rows)], scratch)


def cross_attention(place, text, q_pieces, text_total, order):
    tokens, width = q_pieces[0].shape
    heads = width // HD
    window_rows = sum(block.shape[1] for block in text)
    block_rows = tokens // 2
    spec = pl.BlockSpec((tokens, HD), lambda h, *_: (0, h))
    text_specs = [pl.BlockSpec((2, block.shape[1], HD), lambda h, *_: (0, 0, h)) for block in text]
    rows = 2 * tokens * heads
    return pl.pallas_call(
        functools.partial(cross_kernel, n_text=len(text), text_total=text_total, order=order),
        grid_spec=pltpu.PrefetchScalarGridSpec(
            num_scalar_prefetch=1,
            grid=(heads,),
            in_specs=text_specs + [spec] * 2,
            out_specs=[spec] * 2,
            scratch_shapes=[
                pltpu.VMEM((2, window_rows, HD), BF),
                pltpu.VMEM((HD, text_total), BF),
                pltpu.VMEM((3, block_rows, text_total), F32),
            ],
        ),
        out_shape=[jax.ShapeDtypeStruct((tokens, width), BF)] * 2,
        compiler_params=pltpu.CompilerParams(vmem_limit_bytes=VMEM),
        cost_estimate=pl.CostEstimate(
            flops=rows * text_total * HD * 4 * 2,
            bytes_accessed=4 * tokens * width * 2 + 2 * window_rows * width * 2,
            transcendentals=rows * text_total,
        ),
        name="cross_attention",
    )(place, *text, *q_pieces)


def body(
    q_raw,
    k_raw,
    v_in,
    cross_q_raw,
    text_k_raw,
    text_v,
    q_gain,
    k_gain,
    cross_q_gain,
    text_k_gain,
    nbr,
    nbr_count,
    text_len,
):
    tokens, width = q_raw.shape[1:]
    heads = width // HD
    tiles = nbr.shape[0]
    slots = nbr.shape[1]
    tile = tokens // tiles
    shards = lax.axis_size("frame")
    pairs = shards // 2
    shard = lax.axis_index("frame")
    side = shard % 2
    pair = shard // 2
    cuts = [0, (heads + 1) // 2, heads]
    chunks = [(a * HD, b * HD) for a, b in zip(cuts, cuts[1:])]

    def partner(value):
        return lax.ppermute(value, "frame", [(i, i ^ 1) for i in range(shards)])

    def up(value, least=0):
        moves = [(i, i + 2) for i in range(shards - 2) if i // 2 >= least]
        return lax.ppermute(value, "frame", moves)

    def down(value, least=0):
        moves = [(i, i - 2) for i in range(2, shards) if i // 2 < pairs - least]
        return lax.ppermute(value, "frame", moves)

    def mine(value):
        return lax.dynamic_index_in_dim(value, side, 0, keepdims=False)

    def theirs(value):
        return lax.dynamic_index_in_dim(value, 1 - side, 0, keepdims=False)

    def after(value, *others):
        return lax.optimization_barrier((value, *others))[0]

    meta = jnp.concatenate([nbr, nbr_count[:, None]], axis=1)
    got_meta = partner(meta)
    meta = jnp.concatenate([meta, got_meta], axis=0)
    neighbour, count = meta[:, :slots], meta[:, slots]
    near_shard = neighbour // tiles
    index = (
        (near_shard // 2 - pair + 1) * (2 * tiles)
        + ((near_shard % 2) ^ side) * tiles
        + neighbour % tiles
    )
    index = jnp.clip(index, 0, 6 * tiles - 1).reshape(-1)
    v_keep, v_send = mine(v_in), theirs(v_in)
    v_got = partner(v_send)
    v_up, v_down = up(v_keep), down(v_keep)

    q_late, k_late, cq_late, text_late = (
        after(t, v_keep, v_send) for t in (q_raw, k_raw, cross_q_raw, text_k_raw)
    )
    sums = jnp.concatenate([squares(t) for t in (q_late, k_late, cq_late, text_late)], axis=1)
    totals = lax.psum(sums, "head")
    v_got_up, v_got_down = up(v_got), down(v_got)
    v_pieces = [v_up, v_got_up, v_keep, v_got, v_down, v_got_down]

    text_factor = lax.rsqrt(totals[:, 3 * tokens :] / D + EPSILON)[:, :, None]
    text_keys = (text_k_raw.astype(F32) * text_factor * text_k_gain).astype(BF)
    shard_text = text_keys.shape[1]
    text_total = shard_text * shards
    text_both = jnp.stack([text_keys, text_v], axis=1)
    order = 2 * shard_text
    relayed = pairs <= 4
    if relayed:
        text_got = partner(after(theirs(text_both), v_got))
        text_pair = jnp.concatenate([mine(text_both), text_got], axis=1)
        start, text_side = (pairs - 1 - pair) * order, side
    else:
        gathered = lax.all_gather(text_both, "frame", axis=2, tiled=True)
        text_got = mine(gathered)
        start, text_side = jnp.zeros_like(pair), jnp.zeros_like(side)
    place = jnp.stack([start, text_len[side], text_side]).astype(jnp.int32)

    keep_q, keep_k, keep_cq, send_q, send_k, send_cq = pack(
        jnp.reshape(side, (1,)),
        totals[:, : 3 * tokens].reshape(2, 3, 1, tokens),
        jnp.stack([q_gain, k_gain, cross_q_gain]),
        (q_raw, k_raw, cross_q_raw),
    )
    got_k = partner(after(send_k, text_got, v_up, v_down))
    got_cq = partner(after(send_cq, got_k, got_meta))
    got_q = partner(after(send_q, got_cq))
    cross_pieces = [keep_cq, got_cq]
    q_pieces = [keep_q, got_q]

    if relayed:
        text_pair = after(text_pair, v_up, v_down)
        ups, downs = [text_pair], [text_pair]
        for step in range(pairs - 1):
            ups.append(up(ups[-1], step))
            downs.append(down(downs[-1], step))
        text = ups[:0:-1] + [text_pair] + downs[1:]
    else:
        text = [text_got]
    joined_k = join(keep_k, got_k, chunks)
    k_pieces = []
    for number, own in enumerate(joined_k):
        if number == 0:
            own = after(own, v_got_up, v_got_down)
        own = after(own, *text[max(0, 1 - number) : len(text) - max(0, 1 - number)])
        k_pieces.append([up(own), own, down(own)])

    cross_keep, cross_send = cross_attention(place, text, cross_pieces, text_total, order)
    cross_got = partner(after(cross_send, got_q))
    self_keep, self_got = [], []
    calls = [(0, 0, cuts[1]), (1, cuts[1], heads)]
    for order_of_call, (number, c0, c1) in enumerate(calls):
        waits = [cross_keep, *self_keep]
        waits += [cross_got, *self_got][:order_of_call]
        out_keep, out_send = self_attention(
            index,
            count,
            [after(k, *waits) for k in k_pieces[number]],
            v_pieces,
            q_pieces,
            c0,
            c0 - cuts[number],
            c1 - c0,
            tile,
            slots,
        )
        self_keep.append(out_keep)
        self_got.append(partner(out_send))

    def joined(own, got):
        rows = jnp.arange(2, dtype=jnp.int32)[:, None, None] == side
        return jnp.where(rows, own[None], got[None])

    self_out = jnp.concatenate([joined(a, b) for a, b in zip(self_keep, self_got)], axis=2)
    return (self_out, joined(cross_keep, cross_got))


def solution(mesh):
    in_specs = (
        P(None, "frame", "head"),
        P(None, "frame", "head"),
        P(None, "frame", "head"),
        P(None, "frame", "head"),
        P(None, "frame", "head"),
        P(None, "frame", "head"),
        P("head"),
        P("head"),
        P("head"),
        P("head"),
        P("frame", None),
        P("frame"),
        P(),
    )
    out_specs = (P(None, "frame", "head"), P(None, "frame", "head"))
    return jax.shard_map(body, mesh=mesh, in_specs=in_specs, out_specs=out_specs, check_vma=False)
```

```python
import functools
import math

import jax
import jax.numpy as jnp
from jax import lax
from jax.experimental import pallas as pl
from jax.experimental.pallas import tpu as pltpu
from jax.sharding import PartitionSpec as P

D = 5120
HD = 128
EPSILON = 1e-06
LEAST = 7
FAR = -1e30
SCALE2 = math.log2(math.e) / math.sqrt(HD)
VMEM = 56 * 1024 * 1024
BF = jnp.bfloat16
BRIEF = pl.CostEstimate(flops=0, bytes_accessed=1024, transcendentals=0)
F32 = jnp.float32


def squares(tensor):
    values = tensor.astype(F32)
    return jnp.sum(values * values, axis=-1)


def weigh(stages, scratch):
    held = {}

    def scores(number):
        top, at, spans = None, 0, []
        for block in stages[number][0]:
            score = block()
            width = score.shape[1]
            scratch[number % 3, :, at : at + width] = score
            spans.append((at, width))
            at += width
            for c in range(0, width, 128):
                part = score[:, c : c + 128]
                top = part if top is None else jnp.maximum(top, part)
        held[number] = spans, jnp.max(top, axis=1, keepdims=True)

    def powers(number):
        spans, top = held[number]
        total = None
        for start, width in spans:
            for c in range(start, start + width, 128):
                power = jnp.exp2((scratch[number % 3, :, c : c + 128] - top) * SCALE2)
                scratch[number % 3, :, c : c + 128] = power
                total = power if total is None else total + power
        held[number] = spans, 1.0 / jnp.sum(total, axis=1, keepdims=True)

    def products(number):
        spans, inverse = held[number]
        out = None
        for (start, width), value in zip(spans, stages[number][1]):
            weights = (scratch[number % 3, :, start : start + width] * inverse).astype(BF)
            part = jnp.dot(weights, value(), preferred_element_type=F32)
            out = part if out is None else out + part
        stages[number][2](out.astype(BF))

    for step in range(len(stages) + 2):
        for work, number in ((scores, step), (powers, step - 1), (products, step - 2)):
            if 0 <= number < len(stages):
                work(number)


def pack_kernel(side, totals, gains, *refs):
    raws, outs = refs[:3], refs[3:]
    rows = raws[0].shape[1]
    width = raws[0].shape[2]

    def write(dest):
        for i in range(3):
            row = totals[0, i, :, :]
            factor = lax.rsqrt(row / D + EPSILON)
            column = jnp.transpose(jnp.broadcast_to(factor, (HD, rows)))
            for c in range(0, width, HD):
                value = raws[i][0, :, c : c + HD].astype(F32)
                dest[i][:, c : c + HD] = (value * column * gains[i : i + 1, c : c + HD]).astype(BF)

    @pl.when(pl.program_id(0) == 0)
    def _():
        write(outs[:3])

    @pl.when(pl.program_id(0) == 1)
    def _():
        write(outs[3:])


def pack(side, totals, gains, raws):
    tokens, width = raws[0].shape[1:]
    rows = 128
    steps = tokens // rows

    raw_spec = pl.BlockSpec((1, rows, width), lambda i, t, side_ref: ((side_ref[0] + i) % 2, t, 0))
    total_spec = pl.BlockSpec(
        (1, 3, 1, rows), lambda i, t, side_ref: ((side_ref[0] + i) % 2, 0, 0, t)
    )
    gain_spec = pl.BlockSpec(gains.shape, lambda i, t, side_ref: (0, 0))
    keep_spec = pl.BlockSpec((rows, width), lambda i, t, side_ref: (t * (1 - i) + (steps - 1) * i, 0))
    send_spec = pl.BlockSpec((rows, width), lambda i, t, side_ref: (t * i, 0))
    return pl.pallas_call(
        pack_kernel,
        grid_spec=pltpu.PrefetchScalarGridSpec(
            num_scalar_prefetch=1,
            grid=(2, steps),
            in_specs=[total_spec, gain_spec] + [raw_spec] * 3,
            out_specs=[keep_spec] * 3 + [send_spec] * 3,
        ),
        out_shape=[jax.ShapeDtypeStruct((tokens, width), BF)] * 6,
        compiler_params=pltpu.CompilerParams(vmem_limit_bytes=VMEM),
        cost_estimate=BRIEF,
        name="norm_pack",
    )(side, totals, gains, *raws)


def join_kernel(first, second, *outs, spans):
    for i, ref in enumerate((first, second)):

        @pl.when(pl.program_id(0) == i)
        def _(ref=ref):
            for out, (c0, c1) in zip(outs, spans):
                out[...] = ref[:, c0:c1]


def join(first, second, spans):
    tokens, width = first.shape
    return pl.pallas_call(
        functools.partial(join_kernel, spans=spans),
        grid=(2,),
        in_specs=[pl.BlockSpec((tokens, width), lambda i: (0, 0))] * 2,
        out_specs=[pl.BlockSpec((tokens, c1 - c0), lambda i: (i, 0)) for c0, c1 in spans],
        out_shape=[jax.ShapeDtypeStruct((2 * tokens, c1 - c0), BF) for c0, c1 in spans],
        compiler_params=pltpu.CompilerParams(vmem_limit_bytes=VMEM),
        cost_estimate=BRIEF,
        name="join",
    )(first, second)


def self_kernel(index, count, *refs, tile, slots, n_k, n_v):
    k_pieces, v_pieces = refs[:n_k], refs[n_k : n_k + n_v]
    q_pieces, out_pieces = refs[n_k + n_v : n_k + n_v + 2], refs[n_k + n_v + 2 : n_k + n_v + 4]
    k_window, v_window, scratch = refs[n_k + n_v + 4 :]
    at = 0
    for piece in k_pieces:
        for start in range(0, piece.shape[0], tile):
            k_window[at] = jnp.transpose(piece[start : start + tile, :])
            at += 1
    at = 0
    for piece in v_pieces:
        for start in range(0, piece.shape[0], tile):
            v_window[at] = piece[start : start + tile, :]
            at += 1
    readers = q_pieces[0].shape[0] // tile
    column = lax.broadcasted_iota(jnp.int32, (1, 2 * tile), 1)

    def stage(half, r):
        number = half * readers + r
        live = count[number]
        rows = slice(r * tile, (r + 1) * tile)

        def block(slot):
            pair = [k_window[index[number * slots + slot + i]] for i in range(2)]
            score = jnp.dot(
                q_pieces[half][rows, :],
                jnp.concatenate(pair, axis=1),
                preferred_element_type=F32,
            )
            if slot + 1 >= LEAST:
                score = jnp.where(column < (live - slot) * tile, score, FAR)
            return score

        def value(slot):
            pair = [v_window[index[number * slots + slot + i]] for i in range(2)]
            return jnp.concatenate(pair, axis=0)

        def store(out):
            out_pieces[half][rows, :] = out

        return (
            [functools.partial(block, slot) for slot in range(0, slots, 2)],
            [functools.partial(value, slot) for slot in range(0, slots, 2)],
            store,
        )

    weigh([stage(half, r) for half in range(2) for r in range(readers)], scratch)


def self_attention(index, count, k_pieces, v_pieces, q_pieces, first_head, k_head, heads, tile, slots):
    tokens = q_pieces[0].shape[0]
    width = heads * HD
    window = 6 * tokens // tile

    def spec(piece, base):
        return pl.BlockSpec((piece.shape[0], HD), lambda h, *_: (0, h + base))

    rows = 2 * tokens * heads
    return pl.pallas_call(
        functools.partial(
            self_kernel, tile=tile, slots=slots, n_k=len(k_pieces), n_v=len(v_pieces)
        ),
        grid_spec=pltpu.PrefetchScalarGridSpec(
            num_scalar_prefetch=2,
            grid=(heads,),
            in_specs=[spec(piece, k_head) for piece in k_pieces]
            + [spec(piece, first_head) for piece in (*v_pieces, *q_pieces)],
            out_specs=[pl.BlockSpec((tokens, HD), lambda h, *_: (0, h))] * 2,
            scratch_shapes=[
                pltpu.VMEM((window, HD, tile), BF),
                pltpu.VMEM((window, tile, HD), BF),
                pltpu.VMEM((3, tile, slots * tile), F32),
            ],
        ),
        out_shape=[jax.ShapeDtypeStruct((tokens, width), BF)] * 2,
        compiler_params=pltpu.CompilerParams(vmem_limit_bytes=VMEM),
        cost_estimate=pl.CostEstimate(
            flops=rows * slots * tile * HD * 4 * 2,
            bytes_accessed=16 * tokens * width * 2,
            transcendentals=rows * slots * tile,
        ),
        name="self_attention",
    )(index, count, *k_pieces, *v_pieces, *q_pieces)


def cross_kernel(place, *refs, n_text, text_total, order):
    text = refs[:n_text]
    q_pieces = refs[n_text : n_text + 2]
    out_pieces = refs[n_text + 2 : n_text + 4]
    window, turned, scratch = refs[n_text + 4 :]
    at = 0
    for ref in text:
        rows = ref.shape[1]
        window[:, at : at + rows, :] = ref[...]
        at += rows
    start = pl.multiple_of(place[0], order)
    live = place[1]
    side = place[2]
    tokens = q_pieces[0].shape[0]
    block_rows = scratch.shape[1]
    turned[...] = jnp.transpose(window[0, pl.ds(start, text_total), :])
    column = lax.broadcasted_iota(jnp.int32, (1, text_total), 1)
    half = order // 2
    seen = jnp.where(side == 1, column ^ half, column) < live
    span = 256

    def stage(part, r):
        rows = slice(r * block_rows, (r + 1) * block_rows)

        def block(c):
            score = jnp.dot(
                q_pieces[part][rows, :], turned[:, c : c + span], preferred_element_type=F32
            )
            return jnp.where(seen[:, c : c + span], score, FAR)

        def value(c):
            return window[1, pl.ds(pl.multiple_of(start + c, order), span), :]

        def store(out):
            out_pieces[part][rows, :] = out

        return (
            [functools.partial(block, c) for c in range(0, text_total, span)],
            [functools.partial(value, c) for c in range(0, text_total, span)],
            store,
        )

    weigh([stage(part, r) for part in range(2) for r in range(tokens // block_rows)], scratch)


def cross_attention(place, text, q_pieces, text_total, order):
    tokens, width = q_pieces[0].shape
    heads = width // HD
    window_rows = sum(block.shape[1] for block in text)
    block_rows = tokens // 2
    spec = pl.BlockSpec((tokens, HD), lambda h, *_: (0, h))
    text_specs = [pl.BlockSpec((2, block.shape[1], HD), lambda h, *_: (0, 0, h)) for block in text]
    rows = 2 * tokens * heads
    return pl.pallas_call(
        functools.partial(cross_kernel, n_text=len(text), text_total=text_total, order=order),
        grid_spec=pltpu.PrefetchScalarGridSpec(
            num_scalar_prefetch=1,
            grid=(heads,),
            in_specs=text_specs + [spec] * 2,
            out_specs=[spec] * 2,
            scratch_shapes=[
                pltpu.VMEM((2, window_rows, HD), BF),
                pltpu.VMEM((HD, text_total), BF),
                pltpu.VMEM((3, block_rows, text_total), F32),
            ],
        ),
        out_shape=[jax.ShapeDtypeStruct((tokens, width), BF)] * 2,
        compiler_params=pltpu.CompilerParams(vmem_limit_bytes=VMEM),
        cost_estimate=pl.CostEstimate(
            flops=rows * text_total * HD * 4 * 2,
            bytes_accessed=4 * tokens * width * 2 + 2 * window_rows * width * 2,
            transcendentals=rows * text_total,
        ),
        name="cross_attention",
    )(place, *text, *q_pieces)


def body(
    q_raw,
    k_raw,
    v_in,
    cross_q_raw,
    text_k_raw,
    text_v,
    q_gain,
    k_gain,
    cross_q_gain,
    text_k_gain,
    nbr,
    nbr_count,
    text_len,
):
    tokens, width = q_raw.shape[1:]
    heads = width // HD
    tiles = nbr.shape[0]
    slots = nbr.shape[1]
    tile = tokens // tiles
    shards = lax.axis_size("frame")
    pairs = shards // 2
    shard = lax.axis_index("frame")
    side = shard % 2
    pair = shard // 2
    cuts = [0, (heads + 1) // 2, heads]
    chunks = [(a * HD, b * HD) for a, b in zip(cuts, cuts[1:])]

    def partner(value):
        return lax.ppermute(value, "frame", [(i, i ^ 1) for i in range(shards)])

    def up(value, least=0):
        moves = [(i, i + 2) for i in range(shards - 2) if i // 2 >= least]
        return lax.ppermute(value, "frame", moves)

    def down(value, least=0):
        moves = [(i, i - 2) for i in range(2, shards) if i // 2 < pairs - least]
        return lax.ppermute(value, "frame", moves)

    def mine(value):
        return lax.dynamic_index_in_dim(value, side, 0, keepdims=False)

    def theirs(value):
        return lax.dynamic_index_in_dim(value, 1 - side, 0, keepdims=False)

    def after(value, *others):
        return lax.optimization_barrier((value, *others))[0]

    meta = jnp.concatenate([nbr, nbr_count[:, None]], axis=1)
    got_meta = partner(meta)
    meta = jnp.concatenate([meta, got_meta], axis=0)
    neighbour, count = meta[:, :slots], meta[:, slots]
    near_shard = neighbour // tiles
    index = (
        (near_shard // 2 - pair + 1) * (2 * tiles)
        + ((near_shard % 2) ^ side) * tiles
        + neighbour % tiles
    )
    index = jnp.clip(index, 0, 6 * tiles - 1).reshape(-1)
    v_send = theirs(v_in)
    v_keep = mine(after(v_in, v_send))
    v_got = partner(v_send)
    v_up, v_down = up(v_keep), down(v_keep)

    q_late, k_late, cq_late, text_late = (
        after(t, v_keep, v_send) for t in (q_raw, k_raw, cross_q_raw, text_k_raw)
    )
    sums = jnp.concatenate([squares(t) for t in (q_late, k_late, cq_late, text_late)], axis=1)
    totals = lax.psum(sums, "head")
    v_got_up, v_got_down = up(v_got), down(v_got)
    v_pieces = [v_up, v_got_up, v_keep, v_got, v_down, v_got_down]

    text_factor = lax.rsqrt(totals[:, 3 * tokens :] / D + EPSILON)[:, :, None]
    text_keys = (text_k_raw.astype(F32) * text_factor * text_k_gain).astype(BF)
    shard_text = text_keys.shape[1]
    text_total = shard_text * shards
    text_both = jnp.stack([text_keys, text_v], axis=1)
    order = 2 * shard_text
    relayed = pairs <= 4
    if relayed:
        text_got = partner(after(theirs(text_both), v_got, got_meta))
        text_pair = jnp.concatenate([mine(text_both), text_got], axis=1)
        start, text_side = (pairs - 1 - pair) * order, side
    else:
        gathered = lax.all_gather(text_both, "frame", axis=2, tiled=True)
        text_got = mine(gathered)
        start, text_side = jnp.zeros_like(pair), jnp.zeros_like(side)
    place = jnp.stack([start, text_len[side], text_side]).astype(jnp.int32)

    keep_q, keep_k, keep_cq, send_q, send_k, send_cq = pack(
        jnp.reshape(side, (1,)),
        after(totals[:, : 3 * tokens].reshape(2, 3, 1, tokens), text_got),
        jnp.stack([q_gain, k_gain, cross_q_gain]),
        (q_raw, k_raw, cross_q_raw),
    )
    got_k = partner(after(send_k, text_got, v_up, v_down))
    got_q = partner(after(send_q, got_k, v_got_up, v_got_down))
    got_cq = partner(after(send_cq, got_q))
    cross_pieces = [keep_cq, got_cq]
    q_pieces = [keep_q, got_q]

    if relayed:
        text_pair = after(text_pair, v_up, v_down)
        ups, downs = [text_pair], [text_pair]
        for step in range(pairs - 2):
            ups.append(up(ups[-1], step))
            downs.append(down(downs[-1], step))
    joined_k = join(keep_k, got_k, chunks)

    def spread(own):
        return [up(own), own, down(own)]

    def attend(k_pieces, number, c0, c1, *waits):
        out_keep, out_send = self_attention(
            index,
            count,
            [after(k, *waits) for k in k_pieces] if waits else k_pieces,
            v_pieces,
            q_pieces,
            c0,
            c0 - cuts[number],
            c1 - c0,
            tile,
            slots,
        )
        return out_keep, partner(out_send)

    text_near = (ups[1], downs[1]) if relayed and pairs > 2 else ()
    k_first = spread(after(joined_k[0], v_got_up, v_got_down, *text_near))
    first = attend(k_first, 0, 0, cuts[1])
    if relayed:
        if pairs > 1:
            ups.append(up(after(ups[-1], first[0]), pairs - 2))
            downs.append(down(after(downs[-1], first[0]), pairs - 2))
        inner = ups[-2 if pairs > 2 else -1], downs[-2 if pairs > 2 else -1]
        text = ups[:0:-1] + [text_pair] + downs[1:]
    else:
        inner = ()
        text = [text_got]
    k_second = spread(after(joined_k[1], first[0], *inner))
    cross_keep, cross_send = cross_attention(
        place, text, [after(cross_pieces[0], first[0]), cross_pieces[1]], text_total, order
    )
    cross_got = partner(cross_send)
    split = cuts[1] + (heads - cuts[1] + 1) // 2
    second = attend(k_second, 1, cuts[1], split, cross_keep, first[1])
    third = attend(k_second, 1, split, heads, second[0], cross_got)
    self_keep, self_got = zip(first, second, third)

    def joined(own, got):
        rows = jnp.arange(2, dtype=jnp.int32)[:, None, None] == side
        return jnp.where(rows, own[None], got[None])

    self_out = jnp.concatenate([joined(a, b) for a, b in zip(self_keep, self_got)], axis=2)
    return (self_out, joined(cross_keep, cross_got))


def solution(mesh):
    in_specs = (
        P(None, "frame", "head"),
        P(None, "frame", "head"),
        P(None, "frame", "head"),
        P(None, "frame", "head"),
        P(None, "frame", "head"),
        P(None, "frame", "head"),
        P("head"),
        P("head"),
        P("head"),
        P("head"),
        P("frame", None),
        P("frame"),
        P(),
    )
    out_specs = (P(None, "frame", "head"), P(None, "frame", "head"))
    return jax.shard_map(body, mesh=mesh, in_specs=in_specs, out_specs=out_specs, check_vma=False)
```
